256 devices in a mesh: gx: 32 (over z_lo, y, core), gy: 8 (over z_hi, x).
Axes of the slice: x: 4, y: 4, z: 8 (z_hi: 2, z_lo: 4; z = z_hi * 4 + z_lo), core: 2. Of those that a mesh axis runs over, the one named last changes fastest.
Arguments:
- tsdf: float32 [256, 1024, 1024], P('gx', None, 'gy'), may hold values from -6 to 6
- shift_x: int32 [256], P('gx'), may hold values from -1 to 0
- shift_y: int32 [256], P('gx'), may hold values from -1 to 0
- frac_x: float32 [256], P('gx'), may hold values from 0 to 1
- frac_y: float32 [256], P('gx'), may hold values from 0 to 1
- extinction: float32 [256], P('gx'), may hold values from 0.00390625 to 0.015625
- color_slope: float32 [3], replicated, may hold values from -4 to 4
- color_offset: float32 [3], replicated, may hold values from -3 to 3
- view_mask: int32 [1], replicated, may hold values from 0 to 31
Outputs:
- frame: float32 [4, 1024, 1024], P(None, None, 'gy')
The draws below stay inside these ranges and needn't reach their ends.
Inputs may be any that keep to these rules, and one draw needn't show every extreme that they name: `shift_x`: each entry is -1 or 0. `shift_y`: each entry is -1 or 0.
All inputs are finite; a program needn't handle non-finite values.
Results may differ from the reference program's by a relative error of at most 0.0003.
Values sent between devices are 32-bit elements; how exact they have to be, the bound alone decides.
No kernel may reach another device: no remote copies, remote signals or barrier semaphores. Data moves between devices by JAX's collectives and lax.ppermute only.
A program may use at most 128 MiB of HBM per device.

```python
import math
import jax
import jax.numpy as jnp
from jax import lax

IMG_ROWS = 1024
IMG_COLS = 1024
SLICES = 8
DEPTH = 256
N_GX = 32


def touch_ends(drawn, own_key, smallest, top_value):
    longest = drawn.shape.index(max(drawn.shape))
    spots = []
    for shift in (0, 1):
        where = [jax.random.randint(jax.random.fold_in(own_key, axis), (), 0, length) for axis, length in enumerate(drawn.shape)]
        where[longest] = (where[longest] + shift) % drawn.shape[longest]
        spots.append(tuple(where))
    return drawn.at[spots[0]].set(smallest).at[spots[1]].set(top_value)


def levels(own_key, extent, cuts, smallest, largest):
    def one(position, blocks):
        draws = jax.random.uniform(jax.random.fold_in(jax.random.fold_in(own_key, 6), position), (blocks,), jnp.float32, smallest / len(cuts), largest / len(cuts))
        return jnp.repeat(jnp.exp(draws), extent[position] // blocks).reshape((-1,) + (1,) * (len(extent) - position - 1))

    loudness = one(*cuts[0])
    for cut in cuts[1:]:
        loudness = loudness * one(*cut)
    return loudness


def centred(rng, extent, spread, limit, pieces=(), held_as=jnp.bfloat16):
    drawn = jax.random.normal(rng, extent, jnp.float32) * spread
    if len(pieces) > 0:
        drawn = levels(rng, extent, pieces, -0.22, 0.18) * drawn
    return jnp.clip(drawn, min=-limit, max=limit).astype(held_as)


def setup_inputs(seed: int = 0) -> dict:
    streams_of = jax.random.split(jax.random.key(seed), 10)
    tsdf = centred(streams_of[0], (DEPTH, IMG_ROWS, IMG_COLS), 1.0, 6.0, ((0, 32), (2, 8)), jnp.float32)
    shift_x = touch_ends(jax.random.randint(streams_of[1], (DEPTH,), -1, 1), jax.random.fold_in(streams_of[1], 1), -1, 0).astype(jnp.int32)
    shift_y = touch_ends(jax.random.randint(streams_of[2], (DEPTH,), -1, 1), jax.random.fold_in(streams_of[2], 1), -1, 0).astype(jnp.int32)
    frac_x = jnp.clip(1.0 * jax.random.uniform(streams_of[3], (DEPTH,), jnp.float32) ** levels(streams_of[3], (DEPTH,), ((0, 32),), -0.2, 0.2), 0.0, 1.0)
    frac_y = jnp.clip(1.0 * jax.random.uniform(streams_of[4], (DEPTH,), jnp.float32) ** levels(streams_of[4], (DEPTH,), ((0, 32),), -0.2, 0.2), 0.0, 1.0)
    extinction = jnp.clip(jnp.exp(math.log(0.015625) - 1.3862944 * jax.random.uniform(streams_of[5], (DEPTH,), jnp.float32) ** levels(streams_of[5], (DEPTH,), ((0, 32),), -0.2, 0.2)), 0.00390625, 0.015625)
    color_slope = centred(streams_of[6], (3,), 1.5, 4.0, (), jnp.float32)
    color_offset = centred(streams_of[7], (3,), 1.0, 3.0, (), jnp.float32)
    view_mask = jax.random.randint(streams_of[8], (1,), 0, N_GX).astype(jnp.int32)
    return dict(tsdf=tsdf, shift_x=shift_x, shift_y=shift_y, frac_x=frac_x, frac_y=frac_y, extinction=extinction, color_slope=color_slope, color_offset=color_offset, view_mask=view_mask)


def sample_slice(slab, row_shift, col_shift, row_frac, col_frac):
    row_count = slab.shape[0] - 2
    col_count = slab.shape[1] - 2
    window = lax.dynamic_slice(slab, ((row_shift + 1).astype(jnp.int32), (col_shift + 1).astype(jnp.int32)), (row_count + 1, col_count + 1))
    blended = window[:-1] * (1.0 - row_frac) + window[1:] * row_frac
    return blended[:, :-1] * (1.0 - col_frac) + blended[:, 1:] * col_frac


def render(padded, shift_x, shift_y, frac_x, frac_y, extinction, color_slope, color_offset):
    values = jax.vmap(sample_slice)(padded, shift_x, shift_y, frac_x, frac_y)
    density = jnp.exp(-values * values)
    opacity_step = 1.0 - jnp.exp(-extinction[:, None, None] * density)
    transmit = jnp.cumprod(1.0 - opacity_step, axis=0)
    before = jnp.concatenate([jnp.ones_like(transmit[:1]), transmit[:-1]], axis=0)
    weight = before * opacity_step
    channels = []
    for channel in range(3):
        colour = jax.nn.sigmoid(color_slope[channel] * values + color_offset[channel])
        channels.append(jnp.sum(weight * colour, axis=0))
    channels.append(1.0 - transmit[-1])
    return jnp.stack(channels)


def composite(front, back):
    return front + (1.0 - front[3:4]) * back


def reference(tsdf, shift_x, shift_y, frac_x, frac_y, extinction, color_slope, color_offset, view_mask):
    padded = jnp.pad(tsdf, ((0, 0), (1, 1), (1, 1)))

    def advance(accumulated, order):
        brick = jnp.bitwise_xor(order, view_mask[0]).astype(jnp.int32)
        first = (brick * SLICES).astype(jnp.int32)
        cells = lax.dynamic_slice_in_dim(padded, first, SLICES, 0)
        row_shift = lax.dynamic_slice_in_dim(shift_x, first, SLICES, 0)
        col_shift = lax.dynamic_slice_in_dim(shift_y, first, SLICES, 0)
        row_frac = lax.dynamic_slice_in_dim(frac_x, first, SLICES, 0)
        col_frac = lax.dynamic_slice_in_dim(frac_y, first, SLICES, 0)
        optical = lax.dynamic_slice_in_dim(extinction, first, SLICES, 0)
        partial_value = render(cells, row_shift, col_shift, row_frac, col_frac, optical, color_slope, color_offset)
        return composite(accumulated, partial_value), None

    start = jnp.zeros((4, IMG_ROWS, IMG_COLS), jnp.float32)
    image, _ = lax.scan(advance, start, jnp.arange(N_GX, dtype=jnp.int32))
    return image
```

```python
import functools
import math

import jax
import jax.numpy as jnp
from jax import lax
from jax.experimental import pallas as pl
from jax.experimental.pallas import tpu as pltpu
from jax.sharding import PartitionSpec as P

F32 = jnp.float32
SLICES, ROWS, COLS = 8, 1024, 128
HALF, QUARTER, TILE = 512, 128, 32
STEP = 32
LOG2E = math.log2(math.e)
VMEM = pl.BlockSpec(memory_space=pltpu.VMEM)
SMEM = pl.BlockSpec(memory_space=pltpu.SMEM)
ANY = pl.BlockSpec(memory_space=pl.ANY)
BIG = 48 << 20


def call(kernel, outs, ins, args, scratch=(), cost=1 << 20):
    return pl.pallas_call(
        kernel,
        out_shape=outs,
        in_specs=ins,
        out_specs=jax.tree.map(lambda _: VMEM, outs),
        scratch_shapes=scratch,
        compiler_params=pltpu.CompilerParams(vmem_limit_bytes=BIG),
        cost_estimate=pl.CostEstimate(flops=cost, bytes_accessed=cost, transcendentals=0),
    )(*args)


def image(*shape):
    return jax.ShapeDtypeStruct(shape, F32)


def over(front, back):
    clear = 1.0 - front[3]
    return [front[c] + clear * back[c] for c in range(4)]


def edges_kernel(cells, first, last):
    for k in range(SLICES):
        for r in range(0, 256, 128):
            turned = jnp.transpose(cells[k, r : r + 128, :])
            first[k : k + 1, r : r + 128] = turned[0:1]
            last[k : k + 1, r : r + 128] = turned[127:128]


def edges(tsdf):
    columns = pl.BlockSpec((SLICES, 256), lambda i: (0, i))
    return pl.pallas_call(
        edges_kernel,
        grid=(ROWS // 256,),
        out_shape=[image(SLICES, ROWS)] * 2,
        in_specs=[pl.BlockSpec((SLICES, 256, COLS), lambda i: (0, i, 0))],
        out_specs=[columns, columns],
        compiler_params=pltpu.CompilerParams(vmem_limit_bytes=BIG),
    )(tsdf)


def render_kernel(
    partner, tsdf, left, right, shift_x, shift_y, frac_x, frac_y, extinction, slope, offset, out, cells, side, sems
):
    core = lax.axis_index("gx") & 1
    half = core ^ 1 if partner else core
    base = pl.multiple_of(half * HALF, HALF)
    copies = []
    for c in range(4):
        copies.append(
            pltpu.make_async_copy(
                tsdf.at[:, pl.ds(pl.multiple_of(base + c * 128, 128), 128), :],
                cells.at[:, pl.ds(8 + c * 128, 128), :],
                sems.at[c],
            )
        )
    above = pltpu.make_async_copy(tsdf.at[:, pl.ds(HALF - 8, 8), :], cells.at[:, pl.ds(0, 8), :], sems.at[4])
    below = pltpu.make_async_copy(tsdf.at[:, pl.ds(HALF, 8), :], cells.at[:, pl.ds(HALF + 8, 8), :], sems.at[4])

    @pl.when(half == 1)
    def _():
        above.start()
        cells[:, HALF + 8 :, :] = jnp.zeros((SLICES, 8, COLS), F32)

    @pl.when(half == 0)
    def _():
        below.start()
        cells[:, 0:8, :] = jnp.zeros((SLICES, 8, COLS), F32)

    for copy in copies:
        copy.start()

    row = lax.broadcasted_iota(jnp.int32, (SLICES, ROWS), 1)
    which = lax.broadcasted_iota(jnp.int32, (SLICES, 1), 0)

    def per_slice(ref):
        vec = jnp.zeros((SLICES, 1), F32)
        for k in range(SLICES):
            vec = jnp.where(which == k, ref[k].astype(F32), vec)
        return vec

    sx = per_slice(shift_x)
    sy = per_slice(shift_y)
    fx = per_slice(frac_x)
    mid = jnp.where(sy < -0.5, left[...], right[...])
    prev = jnp.where(row == 0, 0.0, pltpu.roll(mid, 1, 1))
    after = jnp.where(row == ROWS - 1, 0.0, pltpu.roll(mid, ROWS - 1, 1))
    up = sx < -0.5
    blended = jnp.where(up, prev, mid) * (1.0 - fx) + jnp.where(up, mid, after) * fx

    @pl.when(half == 0)
    def _():
        for r in range(0, HALF, 128):
            side[r : r + 128, 0:SLICES] = jnp.transpose(blended[:, r : r + 128])

    @pl.when(half == 1)
    def _():
        for r in range(0, HALF, 128):
            side[r : r + 128, 0:SLICES] = jnp.transpose(blended[:, HALF + r : HALF + r + 128])

    lane = lax.broadcasted_iota(jnp.int32, (STEP, COLS), 1)
    scale = [0.5 * slope[c] for c in range(3)]
    bias = [0.5 * offset[c] for c in range(3)]

    def step(i, carry):
        r = pl.multiple_of(i * STEP, STEP)
        beyond = side[pl.ds(r, STEP), :]
        transmit = jnp.ones((STEP, COLS), F32)
        total = [jnp.zeros((STEP, COLS), F32) for _ in range(3)]
        for k in range(SLICES):
            at = r + 8 + shift_x[k]
            upper = cells[k, pl.ds(at, STEP), :]
            lower = cells[k, pl.ds(at + 1, STEP), :]
            down = frac_x[k]
            mixed = upper * (1.0 - down) + lower * down
            back = shift_y[k] == -1
            turn = jnp.where(back, 1, COLS - 1)
            edge = jnp.where(back, 0, COLS - 1)
            moved = pltpu.roll(mixed, turn, 1)
            moved = jnp.where(lane == edge, beyond[:, k : k + 1], moved)
            far = jnp.where(back, 1.0 - frac_y[k], frac_y[k])
            value = mixed * (1.0 - far) + moved * far
            density = jnp.exp2(value * value * (-LOG2E))
            after = transmit * jnp.exp2(density * (extinction[k] * (-LOG2E)))
            weight = transmit - after
            transmit = after
            for c in range(3):
                total[c] = total[c] + weight * jnp.tanh(value * scale[c] + bias[c])
        alpha = 1.0 - transmit
        for c in range(3):
            out[c, pl.ds(r, STEP), :] = 0.5 * (alpha + total[c])
        out[3, pl.ds(r, STEP), :] = alpha
        return carry

    @pl.when(half == 1)
    def _():
        above.wait()

    @pl.when(half == 0)
    def _():
        below.wait()

    copies[0].wait()
    per = 128 // STEP
    for c in range(4):
        if c < 3:
            copies[c + 1].wait()
        lax.fori_loop(c * per, (c + 1) * per, step, 0)


def render(partner, tsdf, left, right, scalars):
    return call(
        functools.partial(render_kernel, partner),
        image(4, HALF, COLS),
        [ANY, VMEM, VMEM] + [SMEM] * 7,
        (tsdf, left, right, *scalars),
        [
            pltpu.VMEM((SLICES, HALF + 16, COLS), F32),
            pltpu.VMEM((HALF, COLS), F32),
            pltpu.SemaphoreType.DMA((5,)),
        ],
        cost=8 << 20,
    )


def pair_kernel(mask, own, other, here, plus, minus, far):
    index = lax.axis_index("gx")
    y = index >> 1 & 3
    front = (index ^ mask[0]) & 1 == 0
    for away, dest in ((0, here), (1, plus), (3, minus), (2, far)):
        begin = pl.multiple_of(((y + away) & 3) * QUARTER, QUARTER)

        def run(first, second):
            @pl.loop(0, QUARTER, step=TILE)
            def _(r):
                r = pl.multiple_of(r, TILE)
                rows = pl.ds(pl.multiple_of(begin + r, TILE), TILE)
                done = over([first[c, rows, :] for c in range(4)], [second[c, rows, :] for c in range(4)])
                for c in range(4):
                    dest[c, pl.ds(r, TILE), :] = done[c]

        pl.when(front)(functools.partial(run, own, other))
        pl.when(jnp.logical_not(front))(functools.partial(run, other, own))


def pair(mask, own, other):
    return call(
        pair_kernel, [image(4, QUARTER, COLS)] * 4, [SMEM, VMEM, VMEM], (mask, own, other), cost=1 << 20
    )


def in_order(parts, ranks, rows):
    loaded = [[part[c, rows, :] for c in range(4)] for part in parts]
    image_so_far = None
    for place in range(4):
        chosen = loaded[0]
        for part in range(1, 4):
            here = ranks[part] == place
            chosen = [jnp.where(here, loaded[part][c], chosen[c]) for c in range(4)]
        image_so_far = chosen if image_so_far is None else over(image_so_far, chosen)
    return image_so_far


def quarter_kernel(mask, own, plus, minus, far, here, one, two, three):
    index = lax.axis_index("gx")
    y = index >> 1 & 3
    z = index >> 3
    key = mask[0] >> 1 & 3
    ranks = [((y + away) & 3) ^ key for away in (0, 3, 1, 2)]
    for flip, dest in enumerate((here, one, two, three)):
        rows = pl.ds(pl.multiple_of((z ^ flip) * TILE, TILE), TILE)
        done = in_order((own, plus, minus, far), ranks, rows)
        for c in range(4):
            dest[c, :, :] = done[c]


def quarter(mask, parts):
    return call(quarter_kernel, [image(4, TILE, COLS)] * 4, [SMEM] + [VMEM] * 4, (mask, *parts), cost=1 << 19)


def tile_kernel(mask, own, one, two, three, out):
    z = lax.axis_index("gx") >> 3
    key = mask[0] >> 3 & 3
    ranks = [(z ^ flip) ^ key for flip in range(4)]
    done = in_order((own, one, two, three), ranks, pl.ds(0, TILE))
    for c in range(4):
        out[c, :, :] = done[c]


def tile(mask, parts):
    return call(tile_kernel, image(4, TILE, COLS), [SMEM] + [VMEM] * 4, (mask, *parts), cost=1 << 18)


def join_kernel(own, one, two, three, out):
    z = lax.axis_index("gx") >> 3
    for flip, part in enumerate((own, one, two, three)):
        out[:, pl.ds(pl.multiple_of((z ^ flip) * TILE, TILE), TILE), :] = part[...]


def join(parts):
    return call(join_kernel, image(4, QUARTER, COLS), [VMEM] * 4, parts, cost=1 << 19)


def frame_kernel(*refs):
    parts, out, sems = refs[:8], refs[8], refs[9]
    index = lax.axis_index("gx")
    copies = []
    for n, part in enumerate(parts):
        half = index & 1 ^ (n >> 2)
        y = (index >> 1) + (0, 3, 1, 2)[n & 3] & 3
        rows = pl.ds(pl.multiple_of(half * HALF + y * QUARTER, QUARTER), QUARTER)
        copies.append(pltpu.make_async_copy(part, out.at[:, rows, :], sems.at[n]))
    for copy in copies:
        copy.start()
    for copy in copies:
        copy.wait()


def frame(parts):
    return pl.pallas_call(
        frame_kernel,
        out_shape=image(4, ROWS, COLS),
        in_specs=[ANY] * 8,
        out_specs=ANY,
        scratch_shapes=[pltpu.SemaphoreType.DMA((8,))],
    )(*parts)


def send(block, target):
    return lax.ppermute(block, "gx", [(i, target(i)) for i in range(32)])


def flip(bits):
    return lambda i: i ^ bits


def along_y(step):
    return lambda i: i & ~6 | ((i >> 1) + step & 3) << 1


def to_quarters(plus, minus, far):
    return send(plus, along_y(1)), send(minus, along_y(3)), send(far, along_y(2))


def body(tsdf, shift_x, shift_y, frac_x, frac_y, extinction, color_slope, color_offset, view_mask):
    scalars = (shift_x, shift_y, frac_x, frac_y, extinction, color_slope, color_offset)
    first, last = edges(tsdf)
    left = lax.ppermute(last, "gy", [(i, i + 1) for i in range(7)])
    right = lax.ppermute(first, "gy", [(i + 1, i) for i in range(7)])
    given = render(True, tsdf, left, right, scalars)
    other = send(given, flip(1))
    own = render(False, tsdf, left, right, scalars)
    here, plus, minus, far = pair(view_mask, own, other)
    here, one, two, three = quarter(view_mask, (here, *to_quarters(plus, minus, far)))
    mine = tile(view_mask, (here, send(one, flip(8)), send(two, flip(16)), send(three, flip(24))))
    block = join((mine, send(mine, flip(8)), send(mine, flip(16)), send(mine, flip(24))))
    blocks = (block, *to_quarters(block, block, block))
    return frame(blocks + tuple(send(b, flip(1)) for b in blocks))


def solution(mesh):
    in_specs = (P("gx", None, "gy"), P("gx"), P("gx"), P("gx"), P("gx"), P("gx"), P(), P(), P())
    out_specs = P(None, None, "gy")
    return jax.shard_map(body, mesh=mesh, in_specs=in_specs, out_specs=out_specs, check_vma=False)
```

```python
import functools
import math

import jax
import jax.numpy as jnp
from jax import lax
from jax.experimental import pallas as pl
from jax.experimental.pallas import tpu as pltpu
from jax.sharding import PartitionSpec as P

F32 = jnp.float32
SLICES, ROWS, COLS = 8, 1024, 128
HALF, QUARTER, TILE = 512, 128, 32
STEP = 64
CHUNK = 128
AHEAD = 8
PAD = 8
LOG2E = math.log2(math.e)
VMEM = pl.BlockSpec(memory_space=pltpu.VMEM)
SMEM = pl.BlockSpec(memory_space=pltpu.SMEM)
ANY = pl.BlockSpec(memory_space=pl.ANY)
HBM = pl.BlockSpec(memory_space=pltpu.HBM)
BIG = 24 << 20


def call(kernel, outs, ins, args, scratch=(), cost=1 << 20, limit=24 << 20):
    return pl.pallas_call(
        kernel,
        out_shape=outs,
        in_specs=ins,
        out_specs=jax.tree.map(lambda _: VMEM, outs),
        scratch_shapes=scratch,
        compiler_params=pltpu.CompilerParams(vmem_limit_bytes=limit),
        cost_estimate=pl.CostEstimate(flops=cost << 8, bytes_accessed=cost, transcendentals=0),
    )(*args)


def image(*shape):
    return jax.ShapeDtypeStruct(shape, F32)


def over(front, back):
    clear = 1.0 - front[3]
    return [front[c] + clear * back[c] for c in range(4)]


def per_slice(ref):
    which = lax.broadcasted_iota(jnp.int32, (SLICES, 1), 0)
    vec = jnp.zeros((SLICES, 1), F32)
    for k in range(SLICES):
        vec = jnp.where(which == k, ref[k].astype(F32), vec)
    return vec


def edges_kernel(tsdf, cells, columns, to_odd, to_even, block, sems):
    copies = []
    for n in range(ROWS // CHUNK):
        copies.append(
            pltpu.make_async_copy(
                tsdf.at[:, pl.ds(n * CHUNK, CHUNK), :], cells.at[:, pl.ds(PAD + n * CHUNK, CHUNK), :], sems.at[n]
            )
        )
    for copy in copies[:AHEAD]:
        copy.start()
    for r in (0, PAD + ROWS):
        cells[:, r : r + PAD, :] = jnp.zeros((SLICES, PAD, COLS), F32)
    lane = lax.broadcasted_iota(jnp.int32, (128, COLS), 1)
    for n, copy in enumerate(copies):
        copy.wait()
        if n + AHEAD < len(copies):
            copies[n + AHEAD].start()
        for r in range(n * CHUNK, (n + 1) * CHUNK, 128):
            rows = pl.ds(PAD + r, 128)
            packed = pltpu.roll(cells[0, rows, :], 2, 1)
            for k in range(1, SLICES):
                turned = pltpu.roll(cells[k, rows, :], 4 * k + 2, 1)
                packed = jnp.where(lane >= 4 * k, turned, packed)
            block[r // 128] = jnp.transpose(packed)[: 4 * SLICES]
            for j in range(4):
                columns[j, :, r : r + 128] = block[r // 128, pl.ds(j, SLICES, stride=4), :]
    even = lax.axis_index("gy") & 1 == 0
    last, first = columns[1], columns[2]
    to_odd[...] = jnp.where(even, first, last)
    to_even[...] = jnp.where(even, last, first)


def edges(tsdf):
    return call(
        edges_kernel,
        [pltpu.VMEM((SLICES, ROWS + 2 * PAD, COLS), F32), image(4, SLICES, ROWS), image(SLICES, ROWS), image(SLICES, ROWS)],
        [HBM],
        (pltpu.with_memory_space_constraint(tsdf, pltpu.HBM),),
        [
            pltpu.VMEM((ROWS // 128, 4 * SLICES, 128), F32),
            pltpu.SemaphoreType.DMA((ROWS // CHUNK,)),
        ],
        cost=4 << 20,
    )


def border_kernel(
    columns, by_odd, by_even, shift_x, shift_y, frac_x, frac_y, extinction, slope, offset, mine, theirs, whole
):
    even = lax.axis_index("gy") & 1 == 0
    left = jnp.where(even, by_odd[...], by_even[...])
    right = jnp.where(even, by_even[...], by_odd[...])
    row = lax.broadcasted_iota(jnp.int32, (SLICES, ROWS), 1)
    depth = lax.broadcasted_iota(jnp.int32, (SLICES, ROWS), 0)
    up = per_slice(shift_x) < -0.5
    back = per_slice(shift_y) < -0.5
    fx, fy = per_slice(frac_x), per_slice(frac_y)
    optical = per_slice(extinction) * (-LOG2E)
    third, fourth, first, second = (columns[n] for n in range(4))
    pairs = (
        (jnp.where(back, left, first), jnp.where(back, first, second)),
        (jnp.where(back, third, fourth), jnp.where(back, fourth, right)),
    )
    for n, (one, two) in enumerate(pairs):
        mixed = one * (1.0 - fy) + two * fy
        prev = jnp.where(row == 0, 0.0, pltpu.roll(mixed, 1, 1))
        after = jnp.where(row == ROWS - 1, 0.0, pltpu.roll(mixed, ROWS - 1, 1))
        value = jnp.where(up, prev, mixed) * (1.0 - fx) + jnp.where(up, mixed, after) * fx
        passed = jnp.exp2(jnp.exp2(value * value * (-LOG2E)) * optical)
        for far in (1, 2, 4):
            passed = passed * jnp.where(depth >= far, pltpu.roll(passed, far, 0), 1.0)
        weight = jnp.where(depth >= 1, pltpu.roll(passed, 1, 0), 1.0) - passed
        alpha = 1.0 - passed[SLICES - 1 :]
        for c in range(3):
            colour = weight * jnp.tanh(value * (0.5 * slope[c]) + 0.5 * offset[c])
            whole[4 * n + c : 4 * n + c + 1, :] = 0.5 * (alpha + jnp.sum(colour, axis=0, keepdims=True))
        whole[4 * n + 3 : 4 * n + 4, :] = alpha
    core = lax.axis_index("gx") & 1
    mine[...] = whole[:, pl.ds(pl.multiple_of(core * HALF, HALF), HALF)]
    theirs[...] = whole[:, pl.ds(pl.multiple_of((core ^ 1) * HALF, HALF), HALF)]


def border(columns, by_odd, by_even, scalars):
    return call(
        border_kernel,
        [image(8, HALF)] * 2,
        [VMEM] * 3 + [SMEM] * 7,
        (columns, by_odd, by_even, *scalars),
        [pltpu.VMEM((8, ROWS), F32)],
        cost=256 << 20,
    )


def render_kernel(cells, shift_x, shift_y, frac_x, frac_y, extinction, slope, offset, given, own):
    core = lax.axis_index("gx") & 1
    scale = [0.5 * slope[c] for c in range(3)]
    bias = [0.5 * offset[c] for c in range(3)]
    scalars = []
    for k in range(SLICES):
        back = shift_y[k] == -1
        far = jnp.where(back, 1.0 - frac_y[k], frac_y[k])
        near = jnp.where(back, frac_y[k], 1.0 - frac_y[k])
        turn = jnp.where(back, 1, COLS - 1)
        scalars.append((PAD + shift_x[k], 1.0 - frac_x[k], frac_x[k], turn, near, far, extinction[k] * (-LOG2E)))

    def step(out, base, i):
        r = pl.multiple_of(i * STEP, STEP)
        transmit = jnp.ones((STEP, COLS), F32)
        total = [jnp.zeros((STEP, COLS), F32) for _ in range(3)]
        for k in range(SLICES):
            begin, stay, down, turn, near, far, optical = scalars[k]
            upper = cells[k, pl.ds(base + r + begin, STEP), :]
            lower = cells[k, pl.ds(base + r + begin + 1, STEP), :]
            mixed = upper * stay + lower * down
            value = mixed * near + pltpu.roll(mixed, turn, 1) * far
            density = jnp.exp2(value * value * (-LOG2E))
            after = transmit * jnp.exp2(density * optical)
            weight = transmit - after
            transmit = after
            for c in range(3):
                total[c] = total[c] + weight * jnp.tanh(value * scale[c] + bias[c])
        alpha = 1.0 - transmit
        for c in range(3):
            out[c, pl.ds(r, STEP), :] = 0.5 * (alpha + total[c])
        out[3, pl.ds(r, STEP), :] = alpha

    for out, half in ((given, core ^ 1), (own, core)):
        pl.loop(0, HALF // STEP)(functools.partial(step, out, pl.multiple_of(half * HALF, HALF)))


def render(cells, scalars):
    return call(
        render_kernel,
        [image(4, HALF, COLS)] * 2,
        [VMEM] + [SMEM] * 7,
        (cells, *scalars),
        cost=20 << 20,
    )


def pair_kernel(mask, own, other, own_border, other_border, here, plus, minus, far, side):
    index = lax.axis_index("gx")
    y = index >> 1 & 3
    front = (index ^ mask[0]) & 1 == 0
    first = jnp.where(front, own_border[...], other_border[...])
    second = jnp.where(front, other_border[...], own_border[...])
    upper_rows = lax.broadcasted_iota(jnp.int32, (8, HALF), 0) < 4
    merged = first + (1.0 - jnp.where(upper_rows, first[3:4], first[7:8])) * second
    line = lax.broadcasted_iota(jnp.int32, (QUARTER, COLS), 0)
    lane = lax.broadcasted_iota(jnp.int32, (QUARTER, COLS), 1)
    outer = jnp.logical_or(lane == 0, lane == COLS - 1)
    for r in range(0, HALF, QUARTER):
        for c in range(4):
            near, far_side = merged[c : c + 1, r : r + QUARTER], merged[4 + c : 5 + c, r : r + QUARTER]
            side[c, r : r + QUARTER, :] = jnp.transpose(jnp.where(line == 0, near, far_side))
    for away, dest in ((0, here), (1, plus), (3, minus), (2, far)):
        rows = pl.ds(pl.multiple_of((y + away & 3) * QUARTER, QUARTER), QUARTER)

        def run(first, second):
            done = over([first[c, rows, :] for c in range(4)], [second[c, rows, :] for c in range(4)])
            for c in range(4):
                dest[c, :, :] = jnp.where(outer, side[c, rows, :], done[c])

        pl.when(front)(functools.partial(run, own, other))
        pl.when(jnp.logical_not(front))(functools.partial(run, other, own))


def pair(mask, own, other, own_border, other_border):
    return call(
        pair_kernel,
        [image(4, QUARTER, COLS)] * 4,
        [SMEM] + [VMEM] * 4,
        (mask, own, other, own_border, other_border),
        [pltpu.VMEM((4, HALF, COLS), F32)],
    )


def in_order(parts, ranks, rows):
    loaded = [[part[c, rows, :] for c in range(4)] for part in parts]
    image_so_far = None
    for place in range(4):
        chosen = loaded[0]
        for part in range(1, 4):
            here = ranks[part] == place
            chosen = [jnp.where(here, loaded[part][c], chosen[c]) for c in range(4)]
        image_so_far = chosen if image_so_far is None else over(image_so_far, chosen)
    return image_so_far


def quarter_kernel(mask, own, plus, minus, far, here, one, two, three):
    index = lax.axis_index("gx")
    y = index >> 1 & 3
    z = index >> 3
    key = mask[0] >> 1 & 3
    ranks = [((y + away) & 3) ^ key for away in (0, 3, 1, 2)]
    for flip, dest in enumerate((here, one, two, three)):
        rows = pl.ds(pl.multiple_of((z ^ flip) * TILE, TILE), TILE)
        done = in_order((own, plus, minus, far), ranks, rows)
        for c in range(4):
            dest[c, :, :] = done[c]


def quarter(mask, parts):
    return call(quarter_kernel, [image(4, TILE, COLS)] * 4, [SMEM] + [VMEM] * 4, (mask, *parts), cost=1 << 19)


def tile_kernel(mask, own, one, two, three, out):
    z = lax.axis_index("gx") >> 3
    key = mask[0] >> 3 & 3
    ranks = [(z ^ flip) ^ key for flip in range(4)]
    done = in_order((own, one, two, three), ranks, pl.ds(0, TILE))
    for c in range(4):
        out[c, :, :] = done[c]


def tile(mask, parts):
    return call(tile_kernel, image(4, TILE, COLS), [SMEM] + [VMEM] * 4, (mask, *parts), cost=1 << 18)


def join_kernel(own, one, two, three, out):
    z = lax.axis_index("gx") >> 3
    for flip, part in enumerate((own, one, two, three)):
        out[:, pl.ds(pl.multiple_of((z ^ flip) * TILE, TILE), TILE), :] = part[...]


def join(parts):
    return call(join_kernel, image(4, QUARTER, COLS), [VMEM] * 4, parts, cost=1 << 19)


def frame_kernel(*refs):
    parts, out, sems = refs[:8], refs[8], refs[9]
    index = lax.axis_index("gx")
    copies = []
    for n, part in enumerate(parts):
        half = index & 1 ^ (n >> 2)
        y = (index >> 1) + (0, 3, 1, 2)[n & 3] & 3
        rows = pl.ds(pl.multiple_of(half * HALF + y * QUARTER, QUARTER), QUARTER)
        copies.append(pltpu.make_async_copy(part, out.at[:, rows, :], sems.at[n]))
    for copy in copies:
        copy.start()
    for copy in copies:
        copy.wait()


def frame(parts):
    return pl.pallas_call(
        frame_kernel,
        out_shape=image(4, ROWS, COLS),
        in_specs=[VMEM] * 8,
        out_specs=ANY,
        scratch_shapes=[pltpu.SemaphoreType.DMA((8,))],
        compiler_params=pltpu.CompilerParams(vmem_limit_bytes=BIG),
    )(*parts)


def send(block, target):
    return lax.ppermute(block, "gx", [(i, target(i)) for i in range(32)])


def beside(block, first):
    return lax.ppermute(block, "gy", [swap for i in range(first, 7, 2) for swap in ((i, i + 1), (i + 1, i))])


def flip(bits):
    return lambda i: i ^ bits


def along_y(step):
    return lambda i: i & ~6 | ((i >> 1) + step & 3) << 1


def to_quarters(plus, minus, far):
    return send(plus, along_y(1)), send(minus, along_y(3)), send(far, along_y(2))


def body(tsdf, shift_x, shift_y, frac_x, frac_y, extinction, color_slope, color_offset, view_mask):
    scalars = (shift_x, shift_y, frac_x, frac_y, extinction, color_slope, color_offset)
    cells, columns, to_odd, to_even = edges(tsdf)
    by_even = beside(to_even, 0)
    by_odd = beside(to_odd, 1)
    given, own = render(cells, scalars)
    other = send(given, flip(1))
    own, by_odd, by_even = lax.optimization_barrier((own, by_odd, by_even))
    own_border, given_border = border(columns, by_odd, by_even, scalars)
    other_border = send(given_border, flip(1))
    here, plus, minus, far = pair(view_mask, own, other, own_border, other_border)
    here, one, two, three = quarter(view_mask, (here, *to_quarters(plus, minus, far)))
    mine = tile(view_mask, (here, send(one, flip(8)), send(two, flip(16)), send(three, flip(24))))
    block = join((mine, send(mine, flip(8)), send(mine, flip(16)), send(mine, flip(24))))
    blocks = (block, *to_quarters(block, block, block))
    return frame(blocks + tuple(send(b, flip(1)) for b in blocks))


def solution(mesh):
    in_specs = (P("gx", None, "gy"), P("gx"), P("gx"), P("gx"), P("gx"), P("gx"), P(), P(), P())
    out_specs = P(None, None, "gy")
    return jax.shard_map(body, mesh=mesh, in_specs=in_specs, out_specs=out_specs, check_vma=False)
```

```python
import functools
import math

import jax
import jax.numpy as jnp
from jax import lax
from jax.experimental import pallas as pl
from jax.experimental.pallas import tpu as pltpu
from jax.sharding import PartitionSpec as P

F32 = jnp.float32
SLICES, ROWS, COLS = 8, 1024, 128
HALF, QUARTER, TILE = 512, 128, 32
STEP = 512
AWAY = (0, 1, 3, 2)
CHUNK = 256
AHEAD = 4
PAD = 8
LOG2E = math.log2(math.e)
VMEM = pl.BlockSpec(memory_space=pltpu.VMEM)
SMEM = pl.BlockSpec(memory_space=pltpu.SMEM)
ANY = pl.BlockSpec(memory_space=pl.ANY)
HBM = pl.BlockSpec(memory_space=pltpu.HBM)
BIG = 24 << 20


def call(kernel, outs, ins, args, scratch=(), cost=1 << 20, limit=24 << 20):
    return pl.pallas_call(
        kernel,
        out_shape=outs,
        in_specs=ins,
        out_specs=jax.tree.map(lambda _: VMEM, outs),
        scratch_shapes=scratch,
        compiler_params=pltpu.CompilerParams(vmem_limit_bytes=limit),
        cost_estimate=pl.CostEstimate(flops=cost << 8, bytes_accessed=cost, transcendentals=0),
    )(*args)


def image(*shape):
    return jax.ShapeDtypeStruct(shape, F32)


def over(front, back):
    clear = 1.0 - front[3]
    return [front[c] + clear * back[c] for c in range(4)]


def per_slice(ref):
    which = lax.broadcasted_iota(jnp.int32, (SLICES, 1), 0)
    vec = jnp.zeros((SLICES, 1), F32)
    for k in range(SLICES):
        vec = jnp.where(which == k, ref[k].astype(F32), vec)
    return vec


def edges_kernel(tsdf, cells, columns, to_odd, to_even, block, sems):
    copies = []
    for n in range(ROWS // CHUNK):
        copies.append(
            pltpu.make_async_copy(
                tsdf.at[:, pl.ds(n * CHUNK, CHUNK), :], cells.at[:, pl.ds(PAD + n * CHUNK, CHUNK), :], sems.at[n]
            )
        )
    for copy in copies[:AHEAD]:
        copy.start()
    for r in (0, PAD + ROWS):
        cells[:, r : r + PAD, :] = jnp.zeros((SLICES, PAD, COLS), F32)
    lane = lax.broadcasted_iota(jnp.int32, (128, COLS), 1)
    for n, copy in enumerate(copies):
        copy.wait()
        if n + AHEAD < len(copies):
            copies[n + AHEAD].start()
        for r in range(n * CHUNK, (n + 1) * CHUNK, 128):
            rows = pl.ds(PAD + r, 128)
            packed = pltpu.roll(cells[0, rows, :], 2, 1)
            for k in range(1, SLICES):
                turned = pltpu.roll(cells[k, rows, :], 4 * k + 2, 1)
                packed = jnp.where(lane >= 4 * k, turned, packed)
            block[r // 128] = jnp.transpose(packed)[: 4 * SLICES]
            for j in range(4):
                columns[j, :, r : r + 128] = block[r // 128, pl.ds(j, SLICES, stride=4), :]
    even = lax.axis_index("gy") & 1 == 0
    last, first = columns[1], columns[2]
    to_odd[...] = jnp.where(even, first, last)
    to_even[...] = jnp.where(even, last, first)


def edges(tsdf):
    return call(
        edges_kernel,
        [pltpu.VMEM((SLICES, ROWS + 2 * PAD, COLS), F32), image(4, SLICES, ROWS), image(SLICES, ROWS), image(SLICES, ROWS)],
        [HBM],
        (pltpu.with_memory_space_constraint(tsdf, pltpu.HBM),),
        [
            pltpu.VMEM((ROWS // 128, 4 * SLICES, 128), F32),
            pltpu.SemaphoreType.DMA((ROWS // CHUNK,)),
        ],
        cost=4 << 20,
    )


def border_kernel(
    columns, by_odd, by_even, shift_x, shift_y, frac_x, frac_y, extinction, slope, offset, mine, theirs, whole
):
    even = lax.axis_index("gy") & 1 == 0
    left = jnp.where(even, by_odd[...], by_even[...])
    right = jnp.where(even, by_even[...], by_odd[...])
    row = lax.broadcasted_iota(jnp.int32, (SLICES, ROWS), 1)
    depth = lax.broadcasted_iota(jnp.int32, (SLICES, ROWS), 0)
    up = per_slice(shift_x) < -0.5
    back = per_slice(shift_y) < -0.5
    fx, fy = per_slice(frac_x), per_slice(frac_y)
    optical = per_slice(extinction) * (-LOG2E)
    third, fourth, first, second = (columns[n] for n in range(4))
    pairs = (
        (jnp.where(back, left, first), jnp.where(back, first, second)),
        (jnp.where(back, third, fourth), jnp.where(back, fourth, right)),
    )
    for n, (one, two) in enumerate(pairs):
        mixed = one * (1.0 - fy) + two * fy
        prev = jnp.where(row == 0, 0.0, pltpu.roll(mixed, 1, 1))
        after = jnp.where(row == ROWS - 1, 0.0, pltpu.roll(mixed, ROWS - 1, 1))
        value = jnp.where(up, prev, mixed) * (1.0 - fx) + jnp.where(up, mixed, after) * fx
        passed = jnp.exp2(jnp.exp2(value * value * (-LOG2E)) * optical)
        for far in (1, 2, 4):
            passed = passed * jnp.where(depth >= far, pltpu.roll(passed, far, 0), 1.0)
        weight = jnp.where(depth >= 1, pltpu.roll(passed, 1, 0), 1.0) - passed
        alpha = 1.0 - passed[SLICES - 1 :]
        for c in range(3):
            colour = weight * jnp.tanh(value * (0.5 * slope[c]) + 0.5 * offset[c])
            whole[4 * n + c : 4 * n + c + 1, :] = 0.5 * (alpha + jnp.sum(colour, axis=0, keepdims=True))
        whole[4 * n + 3 : 4 * n + 4, :] = alpha
    core = lax.axis_index("gx") & 1
    mine[...] = whole[:, pl.ds(pl.multiple_of(core * HALF, HALF), HALF)]
    theirs[...] = whole[:, pl.ds(pl.multiple_of((core ^ 1) * HALF, HALF), HALF)]


def border(columns, by_odd, by_even, scalars):
    return call(
        border_kernel,
        [image(8, HALF)] * 2,
        [VMEM] * 3 + [SMEM] * 7,
        (columns, by_odd, by_even, *scalars),
        [pltpu.VMEM((8, ROWS), F32)],
        cost=256 << 20,
    )


def render_kernel(cells, shift_x, shift_y, frac_x, frac_y, extinction, slope, offset, given, own):
    core = lax.axis_index("gx") & 1
    scale = [0.5 * slope[c] for c in range(3)]
    bias = [0.5 * offset[c] for c in range(3)]
    scalars = []
    for k in range(SLICES):
        back = shift_y[k] == -1
        far = jnp.where(back, 1.0 - frac_y[k], frac_y[k])
        near = jnp.where(back, frac_y[k], 1.0 - frac_y[k])
        turn = jnp.where(back, 1, COLS - 1)
        scalars.append((PAD + shift_x[k], 1.0 - frac_x[k], frac_x[k], turn, near, far, extinction[k] * (-LOG2E)))

    def step(out, base, i):
        r = pl.multiple_of(i * STEP, STEP)
        transmit = jnp.ones((STEP, COLS), F32)
        total = [jnp.zeros((STEP, COLS), F32) for _ in range(3)]
        for k in range(SLICES):
            begin, stay, down, turn, near, far, optical = scalars[k]
            upper = cells[k, pl.ds(base + r + begin, STEP), :]
            lower = cells[k, pl.ds(base + r + begin + 1, STEP), :]
            mixed = upper * stay + lower * down
            value = mixed * near + pltpu.roll(mixed, turn, 1) * far
            density = jnp.exp2(value * value * (-LOG2E))
            after = transmit * jnp.exp2(density * optical)
            weight = transmit - after
            transmit = after
            for c in range(3):
                total[c] = total[c] + weight * jnp.tanh(value * scale[c] + bias[c])
        alpha = 1.0 - transmit
        for c in range(3):
            out[c, pl.ds(r, STEP), :] = 0.5 * (alpha + total[c])
        out[3, pl.ds(r, STEP), :] = alpha

    for out, half in ((given, core ^ 1), (own, core)):
        pl.loop(0, HALF // STEP)(functools.partial(step, out, pl.multiple_of(half * HALF, HALF)))


def render(cells, scalars):
    return call(
        render_kernel,
        [image(4, HALF, COLS)] * 2,
        [VMEM] + [SMEM] * 7,
        (cells, *scalars),
        cost=20 << 20,
    )


def pair_kernel(mask, own, other, own_border, other_border, *refs):
    dests, side = refs[:8], refs[8]
    index = lax.axis_index("gx")
    y = index >> 1 & 3
    z = index >> 3
    front = (index ^ mask[0]) & 1 == 0
    first = jnp.where(front, own_border[...], other_border[...])
    second = jnp.where(front, other_border[...], own_border[...])
    upper_rows = lax.broadcasted_iota(jnp.int32, (8, HALF), 0) < 4
    merged = first + (1.0 - jnp.where(upper_rows, first[3:4], first[7:8])) * second
    line = lax.broadcasted_iota(jnp.int32, (QUARTER, COLS), 0)
    lane = lax.broadcasted_iota(jnp.int32, (QUARTER, COLS), 1)
    outer = jnp.logical_or(lane == 0, lane == COLS - 1)
    for r in range(0, HALF, QUARTER):
        for c in range(4):
            near, far_side = merged[c : c + 1, r : r + QUARTER], merged[4 + c : 5 + c, r : r + QUARTER]
            side[c, r : r + QUARTER, :] = jnp.transpose(jnp.where(line == 0, near, far_side))
    outer = outer[:TILE]
    for away, rest, single in zip(AWAY, dests[:4], dests[4:]):
        for bits in range(4):
            rows = pl.ds(pl.multiple_of((y + away & 3) * QUARTER + (z ^ bits) * TILE, TILE), TILE)
            dest = rest.at[bits - 1] if bits else single.at[0]

            def run(dest, rows, first, second):
                done = over([first[c, rows, :] for c in range(4)], [second[c, rows, :] for c in range(4)])
                for c in range(4):
                    dest[c, :, :] = jnp.where(outer, side[c, rows, :], done[c])

            pl.when(front)(functools.partial(run, dest, rows, own, other))
            pl.when(jnp.logical_not(front))(functools.partial(run, dest, rows, other, own))


def pair(mask, own, other, own_border, other_border):
    return call(
        pair_kernel,
        [image(3, 4, TILE, COLS)] * 4 + [image(1, 4, TILE, COLS)] * 4,
        [SMEM] + [VMEM] * 4,
        (mask, own, other, own_border, other_border),
        [pltpu.VMEM((4, HALF, COLS), F32)],
    )


def in_order(parts, ranks):
    image_so_far = None
    for place in range(4):
        chosen = parts[0]
        for part in range(1, 4):
            here = ranks[part] == place
            chosen = [jnp.where(here, parts[part][c], chosen[c]) for c in range(4)]
        image_so_far = chosen if image_so_far is None else over(image_so_far, chosen)
    return image_so_far


def along_y_ranks(mask):
    y = lax.axis_index("gx") >> 1 & 3
    return [(y - away & 3) ^ (mask[0] >> 1 & 3) for away in AWAY]


def channels(ref):
    return [ref[c] for c in range(4)]


def quarter_kernel(mask, *refs):
    ranks = along_y_ranks(mask)
    outs = refs[4:]
    for n, out in enumerate(outs):
        done = in_order([channels(ref.at[n]) for ref in refs[:4]], ranks)
        for c in range(4):
            out[c, :, :] = done[c]


def quarter(mask, parts, cost):
    tiles = parts[0].shape[0]
    return call(
        quarter_kernel, [image(4, TILE, COLS)] * tiles, [SMEM] + [VMEM] * 4, (mask, *parts), cost=cost
    )


def tile_kernel(mask, *refs):
    z = lax.axis_index("gx") >> 3
    ranks = [(z ^ bits) ^ (mask[0] >> 3 & 3) for bits in (0, 2, 3, 1)]
    done = in_order([channels(ref) for ref in refs[:4]], ranks)
    for c in range(4):
        refs[4][c, :, :] = done[c]


def tile(mask, parts):
    return call(tile_kernel, image(4, TILE, COLS), [SMEM] + [VMEM] * 4, (mask, *parts))


def join_kernel(*refs):
    for n, part in enumerate(refs[:-1]):
        refs[-1][n] = part[...]


def join(*parts):
    return call(join_kernel, image(len(parts), 4, TILE, COLS), [VMEM] * len(parts), parts, cost=256 << 20)


def frame_kernel(places, *refs):
    parts, out, sems = refs[: len(places)], refs[-2], refs[-1]
    index = lax.axis_index("gx")

    def put(source, side, n, bits):
        y = (index >> 1) - AWAY[n] & 3
        row = (index & 1 ^ side) * HALF + y * QUARTER + (index >> 3 ^ bits) * TILE
        rows = pl.ds(pl.multiple_of(row, TILE), TILE)
        copies.append(pltpu.make_async_copy(source, out.at[:, rows, :], sems.at[len(copies)]))

    copies = []
    for part, (side, n) in zip(parts, places):
        for m in range(part.shape[0]):
            put(part.at[m], side, *((m, 0) if n is None else (n, (2, 3, 1)[m])))
    for copy in copies:
        copy.start()
    for copy in copies:
        copy.wait()


def frame(places, parts, begun=()):
    count = sum(part.shape[0] for part in parts)
    return pl.pallas_call(
        functools.partial(frame_kernel, places),
        out_shape=image(4, ROWS, COLS),
        in_specs=[VMEM] * len(parts) + [ANY] * len(begun),
        out_specs=ANY,
        scratch_shapes=[pltpu.SemaphoreType.DMA((count,))],
        input_output_aliases={len(parts): 0} if begun else {},
        compiler_params=pltpu.CompilerParams(vmem_limit_bytes=BIG),
    )(*parts, *begun)


def send(block, target):
    return lax.ppermute(block, "gx", [(i, target(i)) for i in range(32)])


def beside(block, first):
    return lax.ppermute(block, "gy", [swap for i in range(first, 7, 2) for swap in ((i, i + 1), (i + 1, i))])


def flip(bits):
    return lambda i: i ^ bits


def along_y(step):
    return lambda i: i & ~6 | ((i >> 1) + step & 3) << 1


def along_z(one, two, three):
    two, three, one = send(two, flip(16)), send(three, flip(24)), send(one, flip(8))
    return two, three, one


def to_quarters(plus, minus, far):
    return send(plus, along_y(1)), send(minus, along_y(3)), send(far, along_y(2))


def body(tsdf, shift_x, shift_y, frac_x, frac_y, extinction, color_slope, color_offset, view_mask):
    scalars = (shift_x, shift_y, frac_x, frac_y, extinction, color_slope, color_offset)
    cells, columns, to_odd, to_even = edges(tsdf)
    by_even = beside(to_even, 0)
    by_odd = beside(to_odd, 1)
    given, own = render(cells, scalars)
    other = send(given, flip(1))
    by_odd, by_even, own = lax.optimization_barrier((by_odd, by_even, own))
    own_border, given_border = border(columns, by_odd, by_even, scalars)
    other_border = send(given_border, flip(1))
    pieces = pair(view_mask, own, other, own_border, other_border)
    rests, singles = pieces[:4], pieces[4:]
    came = to_quarters(*rests[1:])
    came_first, *singles = lax.optimization_barrier((came[0], *singles))
    one, two, three = quarter(view_mask, (rests[0], came_first, *came[1:]), 1 << 20)
    over_z = along_z(one, two, three)
    (mine,) = quarter(view_mask, (singles[0], *to_quarters(*singles[1:])), 256 << 20)
    mine = tile(view_mask, (mine, *over_z))
    rest = join(*along_z(mine, mine, mine))
    singles = join(mine, *to_quarters(mine, mine, mine))
    blocks = (singles, rest, *to_quarters(rest, rest, rest))
    others = tuple(send(block, flip(1)) for block in blocks)
    places = [(side, n) for side in range(2) for n in (None, 0, 1, 2, 3)]
    begun = frame(places[:7], blocks + others[:2])
    return frame(places[7:], others[2:], (begun,))


def solution(mesh):
    in_specs = (P("gx", None, "gy"), P("gx"), P("gx"), P("gx"), P("gx"), P("gx"), P(), P(), P())
    out_specs = P(None, None, "gy")
    return jax.shard_map(body, mesh=mesh, in_specs=in_specs, out_specs=out_specs, check_vma=False)
```

```python
import functools
import math

import jax
import jax.numpy as jnp
from jax import lax
from jax.experimental import pallas as pl
from jax.experimental.pallas import tpu as pltpu
from jax.sharding import PartitionSpec as P

F32 = jnp.float32
SLICES, ROWS, COLS = 8, 1024, 128
HALF, QUARTER, TILE = 512, 128, 32
STEP = 512
COST_A = 1 << 16
COST_B = 1 << 16
AWAY = (0, 1, 3, 2)
CHUNK = 256
AHEAD = 4
PAD = 8
LOG2E = math.log2(math.e)
VMEM = pl.BlockSpec(memory_space=pltpu.VMEM)
SMEM = pl.BlockSpec(memory_space=pltpu.SMEM)
ANY = pl.BlockSpec(memory_space=pl.ANY)
HBM = pl.BlockSpec(memory_space=pltpu.HBM)
BIG = 24 << 20


def call(kernel, outs, ins, args, scratch=(), cost=1 << 20, limit=24 << 20):
    return pl.pallas_call(
        kernel,
        out_shape=outs,
        in_specs=ins,
        out_specs=jax.tree.map(lambda _: VMEM, outs),
        scratch_shapes=scratch,
        compiler_params=pltpu.CompilerParams(vmem_limit_bytes=limit),
        cost_estimate=pl.CostEstimate(flops=cost << 8, bytes_accessed=cost, transcendentals=0),
    )(*args)


def image(*shape):
    return jax.ShapeDtypeStruct(shape, F32)


def over(front, back):
    clear = 1.0 - front[3]
    return [front[c] + clear * back[c] for c in range(4)]


def per_slice(ref):
    which = lax.broadcasted_iota(jnp.int32, (SLICES, 1), 0)
    vec = jnp.zeros((SLICES, 1), F32)
    for k in range(SLICES):
        vec = jnp.where(which == k, ref[k].astype(F32), vec)
    return vec


def edges_kernel(tsdf, cells, columns, to_odd, to_even, block, sems):
    copies = []
    for n in range(ROWS // CHUNK):
        copies.append(
            pltpu.make_async_copy(
                tsdf.at[:, pl.ds(n * CHUNK, CHUNK), :], cells.at[:, pl.ds(PAD + n * CHUNK, CHUNK), :], sems.at[n]
            )
        )
    for copy in copies[:AHEAD]:
        copy.start()
    for r in (0, PAD + ROWS):
        cells[:, r : r + PAD, :] = jnp.zeros((SLICES, PAD, COLS), F32)
    lane = lax.broadcasted_iota(jnp.int32, (128, COLS), 1)
    for n, copy in enumerate(copies):
        copy.wait()
        if n + AHEAD < len(copies):
            copies[n + AHEAD].start()
        for r in range(n * CHUNK, (n + 1) * CHUNK, 128):
            rows = pl.ds(PAD + r, 128)
            packed = pltpu.roll(cells[0, rows, :], 2, 1)
            for k in range(1, SLICES):
                turned = pltpu.roll(cells[k, rows, :], 4 * k + 2, 1)
                packed = jnp.where(lane >= 4 * k, turned, packed)
            block[r // 128] = jnp.transpose(packed)[: 4 * SLICES]
            for j in range(4):
                columns[j, :, r : r + 128] = block[r // 128, pl.ds(j, SLICES, stride=4), :]
    even = lax.axis_index("gy") & 1 == 0
    last, first = columns[1], columns[2]
    to_odd[...] = jnp.where(even, first, last)
    to_even[...] = jnp.where(even, last, first)


def edges(tsdf):
    return call(
        edges_kernel,
        [pltpu.VMEM((SLICES, ROWS + 2 * PAD, COLS), F32), image(4, SLICES, ROWS), image(SLICES, ROWS), image(SLICES, ROWS)],
        [HBM],
        (pltpu.with_memory_space_constraint(tsdf, pltpu.HBM),),
        [
            pltpu.VMEM((ROWS // 128, 4 * SLICES, 128), F32),
            pltpu.SemaphoreType.DMA((ROWS // CHUNK,)),
        ],
        cost=4 << 20,
    )


def border_kernel(
    columns, by_odd, by_even, shift_x, shift_y, frac_x, frac_y, extinction, slope, offset, mine, theirs, whole
):
    even = lax.axis_index("gy") & 1 == 0
    left = jnp.where(even, by_odd[...], by_even[...])
    right = jnp.where(even, by_even[...], by_odd[...])
    row = lax.broadcasted_iota(jnp.int32, (SLICES, ROWS), 1)
    depth = lax.broadcasted_iota(jnp.int32, (SLICES, ROWS), 0)
    up = per_slice(shift_x) < -0.5
    back = per_slice(shift_y) < -0.5
    fx, fy = per_slice(frac_x), per_slice(frac_y)
    optical = per_slice(extinction) * (-LOG2E)
    third, fourth, first, second = (columns[n] for n in range(4))
    pairs = (
        (jnp.where(back, left, first), jnp.where(back, first, second)),
        (jnp.where(back, third, fourth), jnp.where(back, fourth, right)),
    )
    for n, (one, two) in enumerate(pairs):
        mixed = one * (1.0 - fy) + two * fy
        prev = jnp.where(row == 0, 0.0, pltpu.roll(mixed, 1, 1))
        after = jnp.where(row == ROWS - 1, 0.0, pltpu.roll(mixed, ROWS - 1, 1))
        value = jnp.where(up, prev, mixed) * (1.0 - fx) + jnp.where(up, mixed, after) * fx
        passed = jnp.exp2(jnp.exp2(value * value * (-LOG2E)) * optical)
        for far in (1, 2, 4):
            passed = passed * jnp.where(depth >= far, pltpu.roll(passed, far, 0), 1.0)
        weight = jnp.where(depth >= 1, pltpu.roll(passed, 1, 0), 1.0) - passed
        alpha = 1.0 - passed[SLICES - 1 :]
        for c in range(3):
            colour = weight * jnp.tanh(value * (0.5 * slope[c]) + 0.5 * offset[c])
            whole[4 * n + c : 4 * n + c + 1, :] = 0.5 * (alpha + jnp.sum(colour, axis=0, keepdims=True))
        whole[4 * n + 3 : 4 * n + 4, :] = alpha
    core = lax.axis_index("gx") & 1
    mine[...] = whole[:, pl.ds(pl.multiple_of(core * HALF, HALF), HALF)]
    theirs[...] = whole[:, pl.ds(pl.multiple_of((core ^ 1) * HALF, HALF), HALF)]


def border(columns, by_odd, by_even, scalars):
    return call(
        border_kernel,
        [image(8, HALF)] * 2,
        [VMEM] * 3 + [SMEM] * 7,
        (columns, by_odd, by_even, *scalars),
        [pltpu.VMEM((8, ROWS), F32)],
        cost=256 << 20,
    )


def render_kernel(cells, shift_x, shift_y, frac_x, frac_y, extinction, slope, offset, given, own):
    core = lax.axis_index("gx") & 1
    scale = [0.5 * slope[c] for c in range(3)]
    bias = [0.5 * offset[c] for c in range(3)]
    scalars = []
    for k in range(SLICES):
        back = shift_y[k] == -1
        far = jnp.where(back, 1.0 - frac_y[k], frac_y[k])
        near = jnp.where(back, frac_y[k], 1.0 - frac_y[k])
        turn = jnp.where(back, 1, COLS - 1)
        scalars.append((PAD + shift_x[k], 1.0 - frac_x[k], frac_x[k], turn, near, far, extinction[k] * (-LOG2E)))

    def step(out, base, i):
        r = pl.multiple_of(i * STEP, STEP)
        transmit = jnp.ones((STEP, COLS), F32)
        total = [jnp.zeros((STEP, COLS), F32) for _ in range(3)]
        for k in range(SLICES):
            begin, stay, down, turn, near, far, optical = scalars[k]
            upper = cells[k, pl.ds(base + r + begin, STEP), :]
            lower = cells[k, pl.ds(base + r + begin + 1, STEP), :]
            mixed = upper * stay + lower * down
            value = mixed * near + pltpu.roll(mixed, turn, 1) * far
            density = jnp.exp2(value * value * (-LOG2E))
            after = transmit * jnp.exp2(density * optical)
            weight = transmit - after
            transmit = after
            for c in range(3):
                total[c] = total[c] + weight * jnp.tanh(value * scale[c] + bias[c])
        alpha = 1.0 - transmit
        for c in range(3):
            out[c, pl.ds(r, STEP), :] = 0.5 * (alpha + total[c])
        out[3, pl.ds(r, STEP), :] = alpha

    for out, half in ((given, core ^ 1), (own, core)):
        pl.loop(0, HALF // STEP)(functools.partial(step, out, pl.multiple_of(half * HALF, HALF)))


def render(cells, scalars):
    return call(
        render_kernel,
        [image(4, HALF, COLS)] * 2,
        [VMEM] + [SMEM] * 7,
        (cells, *scalars),
        cost=20 << 20,
    )


def pair_kernel(mask, own, other, own_border, other_border, *refs):
    dests, side = refs[:8], refs[8]
    index = lax.axis_index("gx")
    y = index >> 1 & 3
    z = index >> 3
    front = (index ^ mask[0]) & 1 == 0
    first = jnp.where(front, own_border[...], other_border[...])
    second = jnp.where(front, other_border[...], own_border[...])
    upper_rows = lax.broadcasted_iota(jnp.int32, (8, HALF), 0) < 4
    merged = first + (1.0 - jnp.where(upper_rows, first[3:4], first[7:8])) * second
    line = lax.broadcasted_iota(jnp.int32, (QUARTER, COLS), 0)
    lane = lax.broadcasted_iota(jnp.int32, (QUARTER, COLS), 1)
    outer = jnp.logical_or(lane == 0, lane == COLS - 1)
    for r in range(0, HALF, QUARTER):
        for c in range(4):
            near, far_side = merged[c : c + 1, r : r + QUARTER], merged[4 + c : 5 + c, r : r + QUARTER]
            side[c, r : r + QUARTER, :] = jnp.transpose(jnp.where(line == 0, near, far_side))
    outer = outer[:TILE]
    for away, early, late in zip(AWAY, dests[:4], dests[4:]):
        for bits in range(4):
            rows = pl.ds(pl.multiple_of((y + away & 3) * QUARTER + (z ^ bits) * TILE, TILE), TILE)
            dest = (early if bits > 1 else late).at[bits & 1]

            def run(dest, rows, first, second):
                done = over([first[c, rows, :] for c in range(4)], [second[c, rows, :] for c in range(4)])
                for c in range(4):
                    dest[c, :, :] = jnp.where(outer, side[c, rows, :], done[c])

            pl.when(front)(functools.partial(run, dest, rows, own, other))
            pl.when(jnp.logical_not(front))(functools.partial(run, dest, rows, other, own))


def pair(mask, own, other, own_border, other_border):
    return call(
        pair_kernel,
        [image(2, 4, TILE, COLS)] * 8,
        [SMEM] + [VMEM] * 4,
        (mask, own, other, own_border, other_border),
        [pltpu.VMEM((4, HALF, COLS), F32)],
    )


def in_order(parts, ranks):
    image_so_far = None
    for place in range(4):
        chosen = parts[0]
        for part in range(1, 4):
            here = ranks[part] == place
            chosen = [jnp.where(here, parts[part][c], chosen[c]) for c in range(4)]
        image_so_far = chosen if image_so_far is None else over(image_so_far, chosen)
    return image_so_far


def along_y_ranks(mask):
    y = lax.axis_index("gx") >> 1 & 3
    return [(y - away & 3) ^ (mask[0] >> 1 & 3) for away in AWAY]


def channels(ref):
    return [ref[c] for c in range(4)]


def quarter_kernel(mask, *refs):
    ranks = along_y_ranks(mask)
    outs = refs[4:]
    for n, out in enumerate(outs):
        done = in_order([channels(ref.at[n]) for ref in refs[:4]], ranks)
        for c in range(4):
            out[c, :, :] = done[c]


def quarter(mask, parts, cost):
    tiles = parts[0].shape[0]
    return call(
        quarter_kernel, [image(4, TILE, COLS)] * tiles, [SMEM] + [VMEM] * 4, (mask, *parts), cost=cost
    )


def tile_kernel(mask, *refs):
    z = lax.axis_index("gx") >> 3
    ranks = [(z ^ bits) ^ (mask[0] >> 3 & 3) for bits in (0, 2, 3, 1)]
    done = in_order([channels(ref) for ref in refs[:4]], ranks)
    for c in range(4):
        refs[4][c, :, :] = done[c]


def tile(mask, parts):
    return call(tile_kernel, image(4, TILE, COLS), [SMEM] + [VMEM] * 4, (mask, *parts))


def join_kernel(*refs):
    begin = 0
    for part in refs[:-1]:
        if len(part.shape) == 3:
            refs[-1][begin] = part[...]
            begin += 1
        else:
            refs[-1][begin : begin + part.shape[0]] = part[...]
            begin += part.shape[0]


def join(*parts):
    count = sum(part.shape[0] if part.ndim == 4 else 1 for part in parts)
    return call(join_kernel, image(count, 4, TILE, COLS), [VMEM] * len(parts), parts, cost=256 << 20)


def frame_kernel(places, *refs):
    parts, out, sems = refs[: len(places)], refs[-2], refs[-1]
    index = lax.axis_index("gx")

    def put(source, side, n, bits):
        y = (index >> 1) - AWAY[n] & 3
        row = (index & 1 ^ side) * HALF + y * QUARTER + (index >> 3 ^ bits) * TILE
        rows = pl.ds(pl.multiple_of(row, TILE), TILE)
        copies.append(pltpu.make_async_copy(source, out.at[:, rows, :], sems.at[len(copies)]))

    copies = []
    for part, (side, upper, n) in zip(parts, places):
        for m in range(part.shape[0]):
            put(part.at[m], side, n, upper + m)
    for copy in copies:
        copy.start()
    for copy in copies:
        copy.wait()


def frame(places, parts, begun=()):
    count = sum(part.shape[0] for part in parts)
    return pl.pallas_call(
        functools.partial(frame_kernel, places),
        out_shape=image(4, ROWS, COLS),
        in_specs=[VMEM] * len(parts) + [ANY] * len(begun),
        out_specs=ANY,
        scratch_shapes=[pltpu.SemaphoreType.DMA((count,))],
        input_output_aliases={len(parts): 0} if begun else {},
        compiler_params=pltpu.CompilerParams(vmem_limit_bytes=BIG),
    )(*parts, *begun)


def send(block, target):
    return lax.ppermute(block, "gx", [(i, target(i)) for i in range(32)])


def beside(block, first):
    return lax.ppermute(block, "gy", [swap for i in range(first, 7, 2) for swap in ((i, i + 1), (i + 1, i))])


def flip(bits):
    return lambda i: i ^ bits


def along_y(step):
    return lambda i: i & ~6 | ((i >> 1) + step & 3) << 1


def to_quarters(plus, minus, far):
    return send(plus, along_y(1)), send(minus, along_y(3)), send(far, along_y(2))


def body(tsdf, shift_x, shift_y, frac_x, frac_y, extinction, color_slope, color_offset, view_mask):
    scalars = (shift_x, shift_y, frac_x, frac_y, extinction, color_slope, color_offset)
    cells, columns, to_odd, to_even = edges(tsdf)
    by_even = beside(to_even, 0)
    by_odd = beside(to_odd, 1)
    given, own = render(cells, scalars)
    other = send(given, flip(1))
    by_odd, by_even, own = lax.optimization_barrier((by_odd, by_even, own))
    own_border, given_border = border(columns, by_odd, by_even, scalars)
    other_border = send(given_border, flip(1))
    pieces = pair(view_mask, own, other, own_border, other_border)
    early, late = pieces[:4], pieces[4:]
    two, three = quarter(view_mask, (early[0], *to_quarters(*early[1:])), COST_A)
    two, three = send(two, flip(16)), send(three, flip(24))
    mine, one = quarter(view_mask, (late[0], *to_quarters(*late[1:])), COST_B)
    one = send(one, flip(8))
    mine = tile(view_mask, (mine, two, three, one))
    near = join(mine, send(mine, flip(8)))
    far = join(send(mine, flip(16)), send(mine, flip(24)))
    blocks = (near, *to_quarters(near, near, near), far, *to_quarters(far, far, far))
    others = tuple(send(block, flip(1)) for block in blocks)
    places = [(side, upper, n) for side in range(2) for upper in (0, 2) for n in range(4)]
    begun = frame(places[:13], blocks + others[:5])
    return frame(places[13:], others[5:], (begun,))


def solution(mesh):
    in_specs = (P("gx", None, "gy"), P("gx"), P("gx"), P("gx"), P("gx"), P("gx"), P(), P(), P())
    out_specs = P(None, None, "gy")
    return jax.shard_map(body, mesh=mesh, in_specs=in_specs, out_specs=out_specs, check_vma=False)
```

```python
import functools
import math

import jax
import jax.numpy as jnp
from jax import lax
from jax.experimental import pallas as pl
from jax.experimental.pallas import tpu as pltpu
from jax.sharding import PartitionSpec as P

F32 = jnp.float32
SLICES, ROWS, COLS = 8, 1024, 128
HALF, QUARTER, TILE = 512, 128, 32
STEP = 512
COST_A = 1 << 16
COST_B = 1 << 16
AWAY = (0, 1, 3, 2)
CHUNK = 256
AHEAD = 4
PAD = 8
LOG2E = math.log2(math.e)
VMEM = pl.BlockSpec(memory_space=pltpu.VMEM)
SMEM = pl.BlockSpec(memory_space=pltpu.SMEM)
ANY = pl.BlockSpec(memory_space=pl.ANY)
HBM = pl.BlockSpec(memory_space=pltpu.HBM)
BIG = 24 << 20


def call(kernel, outs, ins, args, scratch=(), cost=1 << 20, limit=24 << 20):
    return pl.pallas_call(
        kernel,
        out_shape=outs,
        in_specs=ins,
        out_specs=jax.tree.map(lambda _: VMEM, outs),
        scratch_shapes=scratch,
        compiler_params=pltpu.CompilerParams(vmem_limit_bytes=limit),
        cost_estimate=pl.CostEstimate(flops=cost << 8, bytes_accessed=cost, transcendentals=0),
    )(*args)


def image(*shape):
    return jax.ShapeDtypeStruct(shape, F32)


def over(front, back):
    clear = 1.0 - front[3]
    return [front[c] + clear * back[c] for c in range(4)]


def per_slice(ref):
    which = lax.broadcasted_iota(jnp.int32, (SLICES, 1), 0)
    vec = jnp.zeros((SLICES, 1), F32)
    for k in range(SLICES):
        vec = jnp.where(which == k, ref[k].astype(F32), vec)
    return vec


def edges_kernel(tsdf, cells, columns, to_odd, to_even, block, sems):
    copies = []
    for n in range(ROWS // CHUNK):
        copies.append(
            pltpu.make_async_copy(
                tsdf.at[:, pl.ds(n * CHUNK, CHUNK), :], cells.at[:, pl.ds(PAD + n * CHUNK, CHUNK), :], sems.at[n]
            )
        )
    for copy in copies[:AHEAD]:
        copy.start()
    for r in (0, PAD + ROWS):
        cells[:, r : r + PAD, :] = jnp.zeros((SLICES, PAD, COLS), F32)
    lane = lax.broadcasted_iota(jnp.int32, (128, COLS), 1)
    for n, copy in enumerate(copies):
        copy.wait()
        if n + AHEAD < len(copies):
            copies[n + AHEAD].start()
        for r in range(n * CHUNK, (n + 1) * CHUNK, 128):
            rows = pl.ds(PAD + r, 128)
            packed = pltpu.roll(cells[0, rows, :], 2, 1)
            for k in range(1, SLICES):
                turned = pltpu.roll(cells[k, rows, :], 4 * k + 2, 1)
                packed = jnp.where(lane >= 4 * k, turned, packed)
            block[r // 128] = jnp.transpose(packed)[: 4 * SLICES]
            for j in range(4):
                columns[j, :, r : r + 128] = block[r // 128, pl.ds(j, SLICES, stride=4), :]
    even = lax.axis_index("gy") & 1 == 0
    last, first = columns[1], columns[2]
    to_odd[...] = jnp.where(even, first, last)
    to_even[...] = jnp.where(even, last, first)


def edges(tsdf):
    return call(
        edges_kernel,
        [pltpu.VMEM((SLICES, ROWS + 2 * PAD, COLS), F32), image(4, SLICES, ROWS), image(SLICES, ROWS), image(SLICES, ROWS)],
        [HBM],
        (pltpu.with_memory_space_constraint(tsdf, pltpu.HBM),),
        [
            pltpu.VMEM((ROWS // 128, 4 * SLICES, 128), F32),
            pltpu.SemaphoreType.DMA((ROWS // CHUNK,)),
        ],
        cost=4 << 20,
    )


def border_kernel(
    columns, by_odd, by_even, shift_x, shift_y, frac_x, frac_y, extinction, slope, offset, mine, theirs, whole
):
    even = lax.axis_index("gy") & 1 == 0
    left = jnp.where(even, by_odd[...], by_even[...])
    right = jnp.where(even, by_even[...], by_odd[...])
    row = lax.broadcasted_iota(jnp.int32, (SLICES, ROWS), 1)
    depth = lax.broadcasted_iota(jnp.int32, (SLICES, ROWS), 0)
    up = per_slice(shift_x) < -0.5
    back = per_slice(shift_y) < -0.5
    fx, fy = per_slice(frac_x), per_slice(frac_y)
    optical = per_slice(extinction) * (-LOG2E)
    third, fourth, first, second = (columns[n] for n in range(4))
    pairs = (
        (jnp.where(back, left, first), jnp.where(back, first, second)),
        (jnp.where(back, third, fourth), jnp.where(back, fourth, right)),
    )
    for n, (one, two) in enumerate(pairs):
        mixed = one * (1.0 - fy) + two * fy
        prev = jnp.where(row == 0, 0.0, pltpu.roll(mixed, 1, 1))
        after = jnp.where(row == ROWS - 1, 0.0, pltpu.roll(mixed, ROWS - 1, 1))
        value = jnp.where(up, prev, mixed) * (1.0 - fx) + jnp.where(up, mixed, after) * fx
        passed = jnp.exp2(jnp.exp2(value * value * (-LOG2E)) * optical)
        for far in (1, 2, 4):
            passed = passed * jnp.where(depth >= far, pltpu.roll(passed, far, 0), 1.0)
        weight = jnp.where(depth >= 1, pltpu.roll(passed, 1, 0), 1.0) - passed
        alpha = 1.0 - passed[SLICES - 1 :]
        for c in range(3):
            colour = weight * jnp.tanh(value * (0.5 * slope[c]) + 0.5 * offset[c])
            whole[4 * n + c : 4 * n + c + 1, :] = 0.5 * (alpha + jnp.sum(colour, axis=0, keepdims=True))
        whole[4 * n + 3 : 4 * n + 4, :] = alpha
    core = lax.axis_index("gx") & 1
    mine[...] = whole[:, pl.ds(pl.multiple_of(core * HALF, HALF), HALF)]
    theirs[...] = whole[:, pl.ds(pl.multiple_of((core ^ 1) * HALF, HALF), HALF)]


def border(columns, by_odd, by_even, scalars):
    return call(
        border_kernel,
        [image(8, HALF)] * 2,
        [VMEM] * 3 + [SMEM] * 7,
        (columns, by_odd, by_even, *scalars),
        [pltpu.VMEM((8, ROWS), F32)],
        cost=256 << 20,
    )


def render_kernel(cells, shift_x, shift_y, frac_x, frac_y, extinction, slope, offset, given, own):
    core = lax.axis_index("gx") & 1
    scale = [0.5 * slope[c] for c in range(3)]
    bias = [0.5 * offset[c] for c in range(3)]
    scalars = []
    for k in range(SLICES):
        back = shift_y[k] == -1
        far = jnp.where(back, 1.0 - frac_y[k], frac_y[k])
        near = jnp.where(back, frac_y[k], 1.0 - frac_y[k])
        turn = jnp.where(back, 1, COLS - 1)
        scalars.append((PAD + shift_x[k], 1.0 - frac_x[k], frac_x[k], turn, near, far, extinction[k] * (-LOG2E)))

    def step(out, base, i):
        r = pl.multiple_of(i * STEP, STEP)
        transmit = jnp.ones((STEP, COLS), F32)
        total = [jnp.zeros((STEP, COLS), F32) for _ in range(3)]
        for k in range(SLICES):
            begin, stay, down, turn, near, far, optical = scalars[k]
            upper = cells[k, pl.ds(base + r + begin, STEP), :]
            lower = cells[k, pl.ds(base + r + begin + 1, STEP), :]
            mixed = upper * stay + lower * down
            value = mixed * near + pltpu.roll(mixed, turn, 1) * far
            density = jnp.exp2(value * value * (-LOG2E))
            after = transmit * jnp.exp2(density * optical)
            weight = transmit - after
            transmit = after
            for c in range(3):
                total[c] = total[c] + weight * jnp.tanh(value * scale[c] + bias[c])
        alpha = 1.0 - transmit
        for c in range(3):
            out[c, pl.ds(r, STEP), :] = 0.5 * (alpha + total[c])
        out[3, pl.ds(r, STEP), :] = alpha

    for out, half in ((given, core ^ 1), (own, core)):
        pl.loop(0, HALF // STEP)(functools.partial(step, out, pl.multiple_of(half * HALF, HALF)))


def render(cells, scalars):
    return call(
        render_kernel,
        [image(4, HALF, COLS)] * 2,
        [VMEM] + [SMEM] * 7,
        (cells, *scalars),
        cost=20 << 20,
    )


def pair_kernel(mask, own, other, own_border, other_border, *refs):
    dests, side = refs[:8], refs[8]
    index = lax.axis_index("gx")
    y = index >> 1 & 3
    z = index >> 3
    front = (index ^ mask[0]) & 1 == 0
    first = jnp.where(front, own_border[...], other_border[...])
    second = jnp.where(front, other_border[...], own_border[...])
    upper_rows = lax.broadcasted_iota(jnp.int32, (8, HALF), 0) < 4
    merged = first + (1.0 - jnp.where(upper_rows, first[3:4], first[7:8])) * second
    line = lax.broadcasted_iota(jnp.int32, (QUARTER, COLS), 0)
    lane = lax.broadcasted_iota(jnp.int32, (QUARTER, COLS), 1)
    outer = jnp.logical_or(lane == 0, lane == COLS - 1)
    for r in range(0, HALF, QUARTER):
        for c in range(4):
            near, far_side = merged[c : c + 1, r : r + QUARTER], merged[4 + c : 5 + c, r : r + QUARTER]
            side[c, r : r + QUARTER, :] = jnp.transpose(jnp.where(line == 0, near, far_side))
    outer = outer[:TILE]
    for away, early, late in zip(AWAY, dests[:4], dests[4:]):
        for bits in range(4):
            rows = pl.ds(pl.multiple_of((y + away & 3) * QUARTER + (z ^ bits) * TILE, TILE), TILE)
            dest = (early if bits > 1 else late).at[bits & 1]

            def run(dest, rows, first, second):
                done = over([first[c, rows, :] for c in range(4)], [second[c, rows, :] for c in range(4)])
                for c in range(4):
                    dest[c, :, :] = jnp.where(outer, side[c, rows, :], done[c])

            pl.when(front)(functools.partial(run, dest, rows, own, other))
            pl.when(jnp.logical_not(front))(functools.partial(run, dest, rows, other, own))


def pair(mask, own, other, own_border, other_border):
    return call(
        pair_kernel,
        [image(2, 4, TILE, COLS)] * 8,
        [SMEM] + [VMEM] * 4,
        (mask, own, other, own_border, other_border),
        [pltpu.VMEM((4, HALF, COLS), F32)],
    )


def in_order(parts, ranks):
    image_so_far = None
    for place in range(4):
        chosen = parts[0]
        for part in range(1, 4):
            here = ranks[part] == place
            chosen = [jnp.where(here, parts[part][c], chosen[c]) for c in range(4)]
        image_so_far = chosen if image_so_far is None else over(image_so_far, chosen)
    return image_so_far


def along_y_ranks(mask):
    y = lax.axis_index("gx") >> 1 & 3
    return [(y - away & 3) ^ (mask[0] >> 1 & 3) for away in AWAY]


def channels(ref):
    return [ref[c] for c in range(4)]


def quarter_kernel(mask, *refs):
    ranks = along_y_ranks(mask)
    outs = refs[4:]
    for n, out in enumerate(outs):
        done = in_order([channels(ref.at[n]) for ref in refs[:4]], ranks)
        for c in range(4):
            out[c, :, :] = done[c]


def quarter(mask, parts, cost):
    tiles = parts[0].shape[0]
    return call(
        quarter_kernel, [image(4, TILE, COLS)] * tiles, [SMEM] + [VMEM] * 4, (mask, *parts), cost=cost
    )


def tile_kernel(mask, *refs):
    z = lax.axis_index("gx") >> 3
    ranks = [(z ^ bits) ^ (mask[0] >> 3 & 3) for bits in (0, 2, 3, 1)]
    done = in_order([channels(ref) for ref in refs[:4]], ranks)
    for c in range(4):
        refs[4][c, :, :] = done[c]


def tile(mask, parts):
    return call(tile_kernel, image(4, TILE, COLS), [SMEM] + [VMEM] * 4, (mask, *parts))


def join_kernel(*refs):
    begin = 0
    for part in refs[:-1]:
        if len(part.shape) == 3:
            refs[-1][begin] = part[...]
            begin += 1
        else:
            refs[-1][begin : begin + part.shape[0]] = part[...]
            begin += part.shape[0]


def join(*parts, cost=256 << 20):
    count = sum(part.shape[0] if part.ndim == 4 else 1 for part in parts)
    return call(join_kernel, image(count, 4, TILE, COLS), [VMEM] * len(parts), parts, cost=cost)


def frame_kernel(places, *refs):
    parts, out, sems = refs[: len(places)], refs[-2], refs[-1]
    index = lax.axis_index("gx")

    def put(source, side, n, bits):
        y = (index >> 1) - AWAY[n] & 3
        row = (index & 1 ^ side) * HALF + y * QUARTER + (index >> 3 ^ bits) * TILE
        rows = pl.ds(pl.multiple_of(row, TILE), TILE)
        copies.append(pltpu.make_async_copy(source, out.at[:, rows, :], sems.at[len(copies)]))

    copies = []
    for part, (side, upper, n) in zip(parts, places):
        for m in range(part.shape[0]):
            put(part.at[m], side, n, upper + m)
    for copy in copies:
        copy.start()
    for copy in copies:
        copy.wait()


def frame(places, parts, begun=()):
    count = sum(part.shape[0] for part in parts)
    return pl.pallas_call(
        functools.partial(frame_kernel, places),
        out_shape=image(4, ROWS, COLS),
        in_specs=[VMEM] * len(parts) + [ANY] * len(begun),
        out_specs=ANY,
        scratch_shapes=[pltpu.SemaphoreType.DMA((count,))],
        input_output_aliases={len(parts): 0} if begun else {},
        compiler_params=pltpu.CompilerParams(vmem_limit_bytes=BIG),
    )(*parts, *begun)


def send(block, target):
    return lax.ppermute(block, "gx", [(i, target(i)) for i in range(32)])


def beside(block, first):
    return lax.ppermute(block, "gy", [swap for i in range(first, 7, 2) for swap in ((i, i + 1), (i + 1, i))])


def flip(bits):
    return lambda i: i ^ bits


def along_y(step):
    return lambda i: i & ~6 | ((i >> 1) + step & 3) << 1


def to_quarters(plus, minus, far):
    return send(plus, along_y(1)), send(minus, along_y(3)), send(far, along_y(2))


def body(tsdf, shift_x, shift_y, frac_x, frac_y, extinction, color_slope, color_offset, view_mask):
    scalars = (shift_x, shift_y, frac_x, frac_y, extinction, color_slope, color_offset)
    cells, columns, to_odd, to_even = edges(tsdf)
    by_even = beside(to_even, 0)
    by_odd = beside(to_odd, 1)
    given, own = render(cells, scalars)
    other = send(given, flip(1))
    by_odd, by_even, own = lax.optimization_barrier((by_odd, by_even, own))
    own_border, given_border = border(columns, by_odd, by_even, scalars)
    other_border = send(given_border, flip(1))
    pieces = pair(view_mask, own, other, own_border, other_border)
    early, late = pieces[:4], pieces[4:]
    two, three = quarter(view_mask, (early[0], *to_quarters(*early[1:])), COST_A)
    two, three = send(two, flip(16)), send(three, flip(24))
    mine, one = quarter(view_mask, (late[0], *to_quarters(*late[1:])), COST_B)
    one = send(one, flip(8))
    mine = tile(view_mask, (mine, two, three, one))
    near = join(mine, send(mine, flip(8)))
    far = join(send(mine, flip(16)), send(mine, flip(24)))
    own = join(near, far, cost=1 << 10)
    plus, minus, opposite = to_quarters(far, far, far)
    blocks = (own, *to_quarters(near, near, near), plus, opposite, minus)
    others = tuple(send(block, flip(1)) for block in blocks)
    places = [(side, upper, n) for side in range(2) for upper, n in ((0, 0), (0, 1), (0, 2), (0, 3), (2, 1), (2, 3), (2, 2))]
    begun = frame(places[:11], blocks + others[:4])
    return frame(places[11:], others[4:], (begun,))


def solution(mesh):
    in_specs = (P("gx", None, "gy"), P("gx"), P("gx"), P("gx"), P("gx"), P("gx"), P(), P(), P())
    out_specs = P(None, None, "gy")
    return jax.shard_map(body, mesh=mesh, in_specs=in_specs, out_specs=out_specs, check_vma=False)
```
